32 devices in a mesh: gx: 8 (over y, x, core), gy: 4 (over z).
Axes of the slice: x: 2, y: 2, z: 4, core: 2. Of those that a mesh axis runs over, the one named last changes fastest.
Arguments:
- start_block: float32 [8, 8, 512, 512], P(None, None, 'gx', 'gy'), may hold values from -120 to 120
- conductivity: float32 [8, 512, 512], P(None, 'gx', 'gy'), may hold values from 0.5 to 2
- reaction: float32 [8, 512, 512], P(None, 'gx', 'gy'), may hold values from 0.5 to 2
Outputs:
- basis: float32 [40, 8, 512, 512], P(None, None, 'gx', 'gy')
- r_factor: float32 [40, 40], replicated
- first_factor: float32 [40, 40], replicated
The draws below stay inside these ranges and needn't reach their ends.
All inputs are finite; a program needn't handle non-finite values.
Results may differ from the reference program's by a relative error of at most 0.00045.
Values sent between devices are 32-bit elements; how exact they have to be, the bound alone decides.
A program may use at most 128 MiB of HBM per device.

```python
import math
import jax
import jax.numpy as jnp
from jax import lax

RHS = 8
STEPS = 4
NZ = 8
COLS = 40
NX = 512
NY = 512
CELLS = 2097152


def draw_start_block(key, part):
    key_scale = jax.random.fold_in(key, 11)
    key_rough = jax.random.fold_in(key, 12)
    key_common = jax.random.fold_in(key, 13)
    full_shape = (RHS, NZ, NX, NY)
    row_scale = jnp.exp(jax.random.uniform(key_scale, (1, NZ, NX, NY), jnp.float32, 0.0, math.log(10.0)))
    ramp_x = 1.0 + 2.0 * jnp.arange(NX, dtype=jnp.float32).reshape(1, 1, NX, 1) / max(NX - 1, 1)
    rough_part = jnp.clip(jax.random.normal(key_rough, full_shape, jnp.float32), -4.0, 4.0)
    common = jnp.clip(jax.random.normal(key_common, (1, NZ, NX, NY), jnp.float32), -4.0, 4.0)
    return 0.2 * (rough_part + 4.0 * common) * row_scale * ramp_x


def block_scale(key, extent, shards, smallest, largest):
    def one(dim, parts):
        heights = jax.random.uniform(jax.random.fold_in(jax.random.fold_in(key, 6), dim), (parts,), jnp.float32, smallest / len(shards), largest / len(shards))
        return jnp.repeat(jnp.exp(heights), extent[dim] // parts).reshape((-1,) + (1,) * (len(extent) - dim - 1))

    level = one(*shards[0])
    for cut in shards[1:]:
        level = level * one(*cut)
    return level


def setup_inputs(seed: int = 0) -> dict:
    key_list = jax.random.split(jax.random.key(seed), 4)
    return {
        "start_block": draw_start_block(jax.random.fold_in(key_list[3], 71), 0),
        "conductivity": jnp.clip(jnp.exp(math.log(2.0) - 1.3862944 * jax.random.uniform(key_list[1], (NZ, NX, NY), jnp.float32) ** block_scale(key_list[1], (NZ, NX, NY), ((1, 8), (2, 4)), -0.2, 0.2)), 0.5, 2.0),
        "reaction": jnp.clip(jnp.exp(math.log(2.0) - 1.3862944 * jax.random.uniform(key_list[2], (NZ, NX, NY), jnp.float32) ** block_scale(key_list[2], (NZ, NX, NY), ((1, 8), (2, 4)), -0.2, 0.2)), 0.5, 2.0),
    }


center_shift = 7.0
step_scale = 1.0 / 3.0

def apply_basis_map(current, conductivity, reaction):
    running = jnp.zeros_like(current)
    for along_axis, offset in ((2, -1), (2, 1), (3, -1), (3, 1), (1, -1), (1, 1)):
        beside = jnp.roll(current, offset, along_axis)
        weight = 0.5 * (conductivity + jnp.roll(conductivity, offset, along_axis - 1))
        running = running + weight * (current - beside)
    return (reaction * current + running - center_shift * current) * step_scale

def cholesky_pass(matrix, cells_total):
    gram_one = jnp.dot(matrix.astype(jnp.float32), matrix.T.astype(jnp.float32), precision=lax.Precision.HIGHEST, preferred_element_type=jnp.float32) / cells_total
    lower_one = jnp.linalg.cholesky(gram_one)
    solved = jax.scipy.linalg.solve_triangular(lower_one, matrix, lower=True)
    return (solved, lower_one)

def reference(start_block, conductivity, reaction):
    blocks = [start_block]
    for power in range(STEPS):
        blocks.append(apply_basis_map(blocks[-1], conductivity, reaction))
    krylov = jnp.concatenate(blocks, 0).reshape(COLS, CELLS)
    first_q, lower_first = cholesky_pass(krylov, CELLS)
    basis, lower_second = cholesky_pass(first_q, CELLS)
    r_factor = jnp.dot(lower_second.T.astype(jnp.float32), lower_first.T.astype(jnp.float32), precision=lax.Precision.HIGHEST, preferred_element_type=jnp.float32)
    return (basis.reshape(COLS, NZ, NX, NY), r_factor, lower_first.T)
```

```python
import functools

import jax
import jax.numpy as jnp
from jax import lax
from jax.experimental import pallas as pl
from jax.experimental.pallas import tpu as pltpu
from jax.sharding import PartitionSpec as P

STEPS = 4
RHS = 8
NZ = 8
COLS = RHS * (STEPS + 1)
LANES = 128
CENTER_SHIFT = 7.0
THIRD = 1.0 / 3.0
MESH = pl.DeviceIdType.MESH
VM = pl.BlockSpec(memory_space=pltpu.VMEM)
F32 = jnp.float32
BF16 = jnp.bfloat16


def lane_iota(shape):
    return lax.broadcasted_iota(jnp.int32, shape, len(shape) - 1)


def roll(v, shift, axis=1):
    shift = shift % v.shape[axis]
    return v if shift == 0 else pltpu.roll(v, shift, axis)


def pack_kernel(nx, u_ref, c_ref, r_ref, bx, by, bd):
    u2 = u_ref.reshape(RHS * NZ * nx, LANES)
    quad = lane_iota((8, LANES)) // 4
    groups = nx // 4
    tiles = nx // 8

    def group(g, _):
        left = jnp.zeros((8, LANES), F32)
        right = jnp.zeros((8, LANES), F32)
        for j in range(4):
            for z in range(NZ):
                v = u2[pl.ds(z * nx + 4 * g + j, RHS, stride=NZ * nx), :]
                here = quad == 4 * z + j
                left = jnp.where(here, roll(v, 16 * z + 4 * j), left)
                right = jnp.where(here, roll(v, 16 * z + 4 * j + 4), right)
        by[0, g] = left
        by[1, g] = right
        return 0

    lax.fori_loop(0, groups, group, 0)
    for i, ref in enumerate((c_ref, r_ref)):
        for t in range(tiles):
            edge = jnp.zeros((8, LANES), F32)
            for z in range(NZ):
                v = ref[z, 8 * t : 8 * t + 8, :]
                edge = jnp.where(quad == 4 * z + 1, roll(v, 16 * z + 4), edge)
                edge = jnp.where(quad == 4 * z + 2, roll(v, 16 * z + 12), edge)
            by[0, groups + tiles * i + t] = edge
            by[1, groups + tiles * i + t] = edge
    for s in range(2):
        g, t, base = (0, 0, 0) if s == 0 else (groups - 1, tiles - 1, nx - 4)
        for j in range(4):
            for z in range(NZ):
                bx[s, j * 8 + z] = u2[pl.ds(z * nx + base + j, RHS, stride=NZ * nx), :]
        bx[s, 32] = by[0, g]
        bx[s, 33] = by[1, g]
        for z in range(NZ):
            bx[s, 34 + z] = c_ref[z, 8 * t : 8 * t + 8, :]
            bx[s, 42 + z] = r_ref[z, 8 * t : 8 * t + 8, :]
        for i in range(2):
            bx[s, 50 + i] = by[0, groups + tiles * i + t]
        for side in range(2):
            bd[s, side, 0] = by[side, g]
            bd[s, side, 1] = by[0, groups + t]
            bd[s, side, 2] = by[0, groups + tiles + t]


def swap_kernel(gx, gy, bx, by, bd, rx, ry, rd, send, recv):
    mx, my = lax.axis_index("gx"), lax.axis_index("gy")
    xs = (lax.rem(mx + gx - 1, gx), lax.rem(mx + 1, gx))
    ys = (lax.rem(my + gy - 1, gy), lax.rem(my + 1, gy))
    jobs = []
    for s in range(2):
        jobs.append((bx.at[s], rx.at[1 - s], (xs[s], my)))
    for s in range(2):
        jobs.append((by.at[s], ry.at[1 - s], (mx, ys[s])))
    for s in range(2):
        for t in range(2):
            jobs.append((bd.at[s, t], rd.at[1 - s, 1 - t], (xs[s], ys[t])))
    barrier = pltpu.get_barrier_semaphore()
    for _, _, where in jobs:
        pl.semaphore_signal(barrier, inc=1, device_id=where, device_id_type=MESH)
    pl.semaphore_wait(barrier, len(jobs))
    copies = []
    for i, (src, dst, where) in enumerate(jobs):
        copy = pltpu.make_async_remote_copy(
            src_ref=src, dst_ref=dst, send_sem=send.at[i], recv_sem=recv.at[i],
            device_id=where, device_id_type=MESH)
        copy.start()
        copies.append(copy)
    for copy in copies:
        copy.wait()


def split3(a):
    high = a.astype(BF16).astype(F32)
    rest = a - high
    mid = rest.astype(BF16).astype(F32)
    return high, mid, rest - mid


def gram_add(acc, a):
    s = jnp.concatenate(split3(a), 0).astype(BF16)
    acc[...] += lax.dot_general(s, s, (((1,), (1,)), ((), ())), preferred_element_type=F32)


def gram_fold(acc):
    rows = acc[0:COLS, :] + acc[COLS : 2 * COLS, :] + acc[2 * COLS :, :]
    g = rows[:, 0:COLS] + rows[:, COLS : 2 * COLS] + rows[:, 2 * COLS :]
    g = jnp.concatenate([g, jnp.zeros((COLS, LANES - COLS), F32)], 1)
    last = jnp.concatenate([g[32:40], jnp.zeros((8, LANES), F32)], 0)
    return g[0:16] + roll(g[16:32], 40) + roll(last, 80)


def factor(packed, cells):
    g = jnp.concatenate([packed, roll(packed, -40), roll(packed[0:8], -80)], 0) * (1.0 / cells)
    lane = lane_iota((COLS, LANES))
    row = lax.broadcasted_iota(jnp.int32, (COLS, LANES), 0)
    m = jnp.where(lane < COLS, g, jnp.where(lane - 64 == row, 1.0, 0.0))
    row1 = lax.broadcasted_iota(jnp.int32, (COLS, 1), 0)
    for j in range(COLS - 1):
        pivot = m[j : j + 1, :]
        scaled = pivot * (1.0 / m[j : j + 1, j : j + 1])
        f = jnp.where(row1 > j, m[:, j : j + 1], 0.0)
        m = m - f * scaled
    d = jnp.sum(jnp.where(lane == row, m, 0.0), axis=1, keepdims=True)
    m = m * (1.0 / jnp.sqrt(d))
    upper = jnp.where((lane >= row) & (lane < COLS), m, 0.0)
    inverse = jnp.where(lane <= row, roll(m, 64), 0.0)
    return upper[:, :COLS], inverse[:, :COLS]


def stack_left(matrix):
    h, m, l = split3(matrix)
    return jnp.concatenate([h, h, m, m, h, l], 1).astype(BF16)


def times(left, a):
    h, m, l = split3(a)
    hm = jnp.concatenate([h, m], 0).astype(BF16)
    lh = jnp.concatenate([l, h], 0).astype(BF16)
    return jnp.dot(left, jnp.concatenate([hm, hm, lh], 0), preferred_element_type=F32)


def across(ref, i):
    return jnp.concatenate([ref[i, z] for z in range(NZ)], 1)


def power_kernel(nx, u_ref, c_ref, r_ref, by, rx, ry, rd, kb, gp, cb, rb, w, cs, sw, sb, acc):
    ext = nx + 8
    groups = nx // 4
    tiles = nx // 8
    lane = lane_iota((8, LANES))
    lane1 = lane_iota((1, LANES))
    sub = (lane % 16) // 4
    u2 = u_ref.reshape(RHS * NZ * nx, LANES)
    c2 = c_ref.reshape(NZ * nx, LANES)
    r2 = r_ref.reshape(NZ * nx, LANES)
    rx2 = rx.reshape(2 * 52 * 8, LANES)
    W = THIRD * 0.5

    for i, dst in ((0, cb), (1, rb)):
        for k in range(4):
            base = (34 + 8 * i) * 8
            dst[k] = rx2[pl.ds(base + 4 + k, 8, stride=8), :]
            dst[nx + 4 + k] = rx2[pl.ds(52 * 8 + base + k, 8, stride=8), :]

    def coef(x, _):
        cb[x + 4] = c2[pl.ds(x, 8, stride=nx), :]
        rb[x + 4] = r2[pl.ds(x, 8, stride=nx), :]
        for z in range(NZ):
            kb[x + 4, z, 0:RHS, :] = u2[pl.ds(z * nx + x, RHS, stride=NZ * nx), :]
        return 0

    lax.fori_loop(0, nx, coef, 0)
    for j in range(4):
        for z in range(NZ):
            kb[j, z, 0:RHS, :] = rx[0, j * 8 + z]
            kb[nx + 4 + j, z, 0:RHS, :] = rx[1, j * 8 + z]

    w[1, 0] = (cb[0] + cb[1]) * W

    def weight(x, _):
        c = cb[x]
        xp = (c + cb[x + 1]) * W
        zp = (c + roll(c, -1, 0)) * W
        yp = jnp.where(lane == LANES - 1, 0.0, (c + roll(c, -1)) * W)
        zm, ym = roll(zp, 1, 0), roll(yp, 1)
        xm = w[1, x - 1]
        w[0, x] = (rb[x] - CENTER_SHIFT) * THIRD + (xp + xm + zp + zm + yp + ym)
        w[1, x] = xp
        w[2, x] = yp
        w[3, x] = ym
        w[4, x] = zp
        w[5, x] = zm
        return 0

    lax.fori_loop(1, ext - 1, weight, 0)

    for i in range(2):
        cs[i, 0:8, :] = jnp.zeros((8, LANES), F32)
        cs[i, nx + 24 : nx + 32, :] = jnp.zeros((8, LANES), F32)
        for t in range(tiles + 2):
            if t == 0 or t == tiles + 1:
                s = 0 if t == 0 else 1
                own, left, right = rx[s, 50 + i], rd[s, 0, 1 + i], rd[s, 1, 1 + i]
            else:
                at = groups + tiles * i + t - 1
                own, left, right = by[0, at], ry[0, at], ry[1, at]
            cs[i, 8 + 8 * t : 16 + 8 * t, :] = jnp.where(
                sub == 0, roll(left, -8), jnp.where(sub == 3, roll(right, 8), own))
    for t in range(tiles + 2):
        a = 8 + 8 * t
        c = cs[0, a : a + 8, :]
        xp = (c + cs[0, a + 1 : a + 9, :]) * W
        xm = (c + cs[0, a - 1 : a + 7, :]) * W
        yp, ym = (c + roll(c, -1)) * W, (c + roll(c, 1)) * W
        zp, zm = (c + roll(c, -16)) * W, (c + roll(c, 16)) * W
        total = xp + xm + zp + zm + yp + ym
        sw[0, a : a + 8, :] = (cs[1, a : a + 8, :] - CENTER_SHIFT) * THIRD + total
        for k, value in enumerate((xp, xm, yp, ym, zp, zm)):
            sw[1 + k, a : a + 8, :] = value

    def strip(g, parts):
        left, own_left, own_right, right = parts
        for j in range(4):
            v = jnp.where(sub == 0, roll(left, -4 * j), roll(own_left, 4 - 4 * j))
            v = jnp.where(sub == 2, roll(own_right, 8 - 4 * j), v)
            sb[0, 4 * g + j] = jnp.where(sub == 3, roll(right, 12 - 4 * j), v)

    strip(0, (rd[0, 0, 0], rx[0, 32], rx[0, 33], rd[0, 1, 0]))
    strip(groups + 1, (rd[1, 0, 0], rx[1, 32], rx[1, 33], rd[1, 1, 0]))

    def strips(g, _):
        strip(g, (ry[0, g - 1], by[0, g - 1], by[1, g - 1], ry[1, g - 1]))
        return 0

    lax.fori_loop(1, groups + 1, strips, 0)

    acc[...] = jnp.zeros_like(acc)
    edge = (lane == 0) | (lane == LANES - 1)
    for p in range(1, STEPS + 1):
        lo, hi = RHS * (p - 1), RHS * p

        def row(x, _):
            s = sb[p - 1, x]

            def strip_weight(k):
                return sw[k, pl.ds(x + 12, 1), :]

            sr, sl = roll(s, -1), roll(s, 1)
            wr, wl = strip_weight(3), strip_weight(4)
            flux = jnp.where(lane % 16 == 11, wr * (sr - s), roll(wl * (sl - s), 8))
            if p < STEPS:
                sb[p, x] = (
                    strip_weight(0) * s
                    - strip_weight(1) * sb[p - 1, x + 1]
                    - strip_weight(2) * sb[p - 1, x - 1]
                    - wr * sr - wl * sl
                    - strip_weight(5) * roll(s, -16)
                    - strip_weight(6) * roll(s, 16))
            cen = [kb[x, z, lo:hi, :] for z in range(NZ)]
            for z in range(NZ):
                c = cen[z]

                def wt(k, at):
                    return w[k, at, z : z + 1, :]

                new = wt(0, x) * c
                new = new - wt(1, x) * kb[x + 1, z, lo:hi, :]
                new = new - wt(1, x - 1) * kb[x - 1, z, lo:hi, :]
                new = new - wt(2, x) * roll(c, -1)
                new = new - wt(3, x) * roll(c, 1)
                new = new - wt(4, x) * cen[(z + 1) % NZ]
                new = new - wt(5, x) * cen[(z - 1) % NZ]
                new = new - jnp.where(edge, roll(flux, 116 - 16 * z), 0.0)
                kb[x, z, hi : hi + RHS, :] = new
            if p == STEPS:
                gram_add(acc, across(kb, x))
            return 0

        lax.fori_loop(p, ext - p, row, 0)
    gp[...] = gram_fold(acc)


def sum_kernel(gx, gy, g_ref, out, bufx, bufy, sx, rx, sy, ry):
    mx, my = lax.axis_index("gx"), lax.axis_index("gy")
    barrier = pltpu.get_barrier_semaphore()
    xs = [lax.rem(mx + d, gx) for d in range(1, gx)]
    ys = [lax.rem(my + d, gy) for d in range(1, gy)]
    for x in xs:
        pl.semaphore_signal(barrier, inc=1, device_id=(x, my), device_id_type=MESH)
    for y in ys:
        pl.semaphore_signal(barrier, inc=1, device_id=(mx, y), device_id_type=MESH)
    pl.semaphore_wait(barrier, len(xs) + len(ys))

    def stage(source, buf, send, recv, me, n, peers, where):
        copies = []
        for i, peer in enumerate(peers):
            copy = pltpu.make_async_remote_copy(
                src_ref=source, dst_ref=buf.at[me], send_sem=send.at[i],
                recv_sem=recv.at[i], device_id=where(peer), device_id_type=MESH)
            copy.start()
            copies.append(copy)
        buf[me] = source[...]
        for copy in copies:
            copy.wait()
        total = buf[0]
        for i in range(1, n):
            total = total + buf[i]
        return total

    out[...] = stage(g_ref, bufx, sx, rx, mx, gx, xs, lambda x: (x, my))
    out[...] = stage(out, bufy, sy, ry, my, gy, ys, lambda y: (mx, y))


def all_sum(packed, gx, gy, cid):
    return pl.pallas_call(
        functools.partial(sum_kernel, gx, gy),
        out_shape=jax.ShapeDtypeStruct(packed.shape, F32),
        in_specs=[VM],
        out_specs=VM,
        scratch_shapes=[
            pltpu.VMEM((gx,) + packed.shape, F32),
            pltpu.VMEM((gy,) + packed.shape, F32),
            pltpu.SemaphoreType.DMA((gx - 1,)),
            pltpu.SemaphoreType.DMA((gx - 1,)),
            pltpu.SemaphoreType.DMA((gy - 1,)),
            pltpu.SemaphoreType.DMA((gy - 1,)),
        ],
        compiler_params=pltpu.CompilerParams(collective_id=cid, has_side_effects=True),
        name=f"sum_{cid}",
    )(packed)


def again_kernel(cells, steps, g_ref, k_ref, upper, inverse, gp, left, acc):
    i = pl.program_id(0)

    @pl.when(i == 0)
    def _():
        up, inv = factor(g_ref[...], cells)
        upper[...] = up
        inverse[...] = inv
        left[...] = stack_left(inv)
        acc[...] = jnp.zeros_like(acc)

    for x in range(k_ref.shape[0]):
        gram_add(acc, times(left[...], across(k_ref, x)))

    @pl.when(i == steps - 1)
    def _():
        gp[...] = gram_fold(acc)


def basis_kernel(cells, g_ref, up_ref, inv_ref, ka, kc, out, r_out, left):
    @pl.when(pl.program_id(0) == 0)
    def _():
        up, inv = factor(g_ref[...], cells)
        r_out[...] = jnp.dot(up, up_ref[...], precision=lax.Precision.HIGHEST, preferred_element_type=F32)
        both = jnp.dot(inv, inv_ref[...], precision=lax.Precision.HIGHEST, preferred_element_type=F32)
        left[...] = stack_left(both)

    flat = out.reshape(COLS * NZ * 8, LANES)
    for x in range(8):
        ref = ka if x < 4 else kc
        q = times(left[...], across(ref, x % 4))
        for z in range(NZ):
            for b in range(COLS // 8):
                flat[pl.ds(b * 8 * NZ * 8 + z * 8 + x, 8, stride=NZ * 8), :] = q[
                    8 * b : 8 * b + 8, LANES * z : LANES * (z + 1)]


def body(start_block, conductivity, reaction):
    gx, gy = lax.axis_size("gx"), lax.axis_size("gy")
    nx = start_block.shape[2]
    ext = nx + 8
    cells = NZ * nx * LANES * gx * gy
    sds = lambda *s: jax.ShapeDtypeStruct(s, F32)
    shapes = [sds(2, 52, 8, LANES), sds(2, nx // 4 + nx // 4, 8, LANES), sds(2, 2, 3, 8, LANES)]
    big = pltpu.CompilerParams(vmem_limit_bytes=48 * 2**20)
    bx, by, bd = pl.pallas_call(
        functools.partial(pack_kernel, nx), out_shape=shapes,
        in_specs=[VM] * 3, out_specs=[VM] * 3, compiler_params=big, name="pack",
    )(start_block, conductivity, reaction)
    rx, ry, rd = pl.pallas_call(
        functools.partial(swap_kernel, gx, gy), out_shape=shapes,
        in_specs=[VM] * 3, out_specs=[VM] * 3,
        scratch_shapes=[pltpu.SemaphoreType.DMA((8,)), pltpu.SemaphoreType.DMA((8,))],
        compiler_params=pltpu.CompilerParams(collective_id=0, has_side_effects=True), name="swap",
    )(bx, by, bd)
    kb, gp = pl.pallas_call(
        functools.partial(power_kernel, nx),
        out_shape=[sds(ext, NZ, COLS, LANES), sds(16, LANES)],
        in_specs=[VM] * 7, out_specs=[VM] * 2,
        scratch_shapes=[
            pltpu.VMEM((ext, 8, LANES), F32),
            pltpu.VMEM((ext, 8, LANES), F32),
            pltpu.VMEM((6, ext, 8, LANES), F32),
            pltpu.VMEM((2, nx + 32, LANES), F32),
            pltpu.VMEM((7, nx + 32, LANES), F32),
            pltpu.VMEM((STEPS, ext, 8, LANES), F32),
            pltpu.VMEM((3 * COLS, 3 * COLS), F32),
        ],
        compiler_params=big, name="powers",
    )(start_block, conductivity, reaction, by, rx, ry, rd)
    total = all_sum(gp, gx, gy, 1)

    whole = lambda *s: pl.BlockSpec(s, lambda i: (0,) * len(s))
    kblock = lambda f: pl.BlockSpec((4, NZ, COLS, LANES), lambda i: (f(i), 0, 0, 0))
    steps = nx // 4
    upper, inverse, gp2 = pl.pallas_call(
        functools.partial(again_kernel, cells, steps),
        grid=(steps,),
        out_shape=[sds(COLS, COLS), sds(COLS, COLS), sds(16, LANES)],
        in_specs=[whole(16, LANES), kblock(lambda i: i + 1)],
        out_specs=[whole(COLS, COLS), whole(COLS, COLS), whole(16, LANES)],
        scratch_shapes=[pltpu.VMEM((COLS, 6 * COLS), BF16), pltpu.VMEM((3 * COLS, 3 * COLS), F32)],
        compiler_params=big, name="again",
    )(total, kb)
    total2 = all_sum(gp2, gx, gy, 2)
    basis, r_factor = pl.pallas_call(
        functools.partial(basis_kernel, cells),
        grid=(nx // 8,),
        out_shape=[sds(COLS, NZ, nx, LANES), sds(COLS, COLS)],
        in_specs=[whole(16, LANES), whole(COLS, COLS), whole(COLS, COLS),
                  kblock(lambda i: 2 * i + 1), kblock(lambda i: 2 * i + 2)],
        out_specs=[pl.BlockSpec((COLS, NZ, 8, LANES), lambda i: (0, 0, i, 0)), whole(COLS, COLS)],
        scratch_shapes=[pltpu.VMEM((COLS, 6 * COLS), BF16)],
        compiler_params=big, name="basis",
    )(total2, upper, inverse, kb, kb)
    return basis, r_factor, upper


def solution(mesh):
    return jax.shard_map(
        body,
        mesh=mesh,
        in_specs=(P(None, None, "gx", "gy"), P(None, "gx", "gy"), P(None, "gx", "gy")),
        out_specs=(P(None, None, "gx", "gy"), P(), P()),
        check_vma=False,
    )
```

```python
import functools

import jax
import jax.numpy as jnp
from jax import lax
from jax.experimental import pallas as pl
from jax.experimental.pallas import tpu as pltpu
from jax.sharding import PartitionSpec as P

STEPS = 4
RHS = 8
NZ = 8
COLS = RHS * (STEPS + 1)
LANES = 128
CENTER_SHIFT = 7.0
THIRD = 1.0 / 3.0
MESH = pl.DeviceIdType.MESH
VM = pl.BlockSpec(memory_space=pltpu.VMEM)
F32 = jnp.float32
BF16 = jnp.bfloat16


def lane_iota(shape):
    return lax.broadcasted_iota(jnp.int32, shape, len(shape) - 1)


def roll(v, shift, axis=1):
    shift = shift % v.shape[axis]
    return v if shift == 0 else pltpu.roll(v, shift, axis)


def pack_kernel(nx, u_ref, c_ref, r_ref, bx, by, bd):
    u2 = u_ref.reshape(RHS * NZ * nx, LANES)
    quad = lane_iota((8, LANES)) // 4
    groups = nx // 4
    tiles = nx // 8

    def group(g, _):
        left = jnp.zeros((8, LANES), F32)
        right = jnp.zeros((8, LANES), F32)
        for j in range(4):
            for z in range(NZ):
                v = u2[pl.ds(z * nx + 4 * g + j, RHS, stride=NZ * nx), :]
                here = quad == 4 * z + j
                left = jnp.where(here, roll(v, 16 * z + 4 * j), left)
                right = jnp.where(here, roll(v, 16 * z + 4 * j + 4), right)
        by[0, g] = left
        by[1, g] = right
        return 0

    lax.fori_loop(0, groups, group, 0)
    for i, ref in enumerate((c_ref, r_ref)):
        for t in range(tiles):
            edge = jnp.zeros((8, LANES), F32)
            for z in range(NZ):
                v = ref[z, 8 * t : 8 * t + 8, :]
                edge = jnp.where(quad == 4 * z + 1, roll(v, 16 * z + 4), edge)
                edge = jnp.where(quad == 4 * z + 2, roll(v, 16 * z + 12), edge)
            by[0, groups + tiles * i + t] = edge
            by[1, groups + tiles * i + t] = edge
    for s in range(2):
        g, t, base = (0, 0, 0) if s == 0 else (groups - 1, tiles - 1, nx - 4)
        for j in range(4):
            for z in range(NZ):
                bx[s, j * 8 + z] = u2[pl.ds(z * nx + base + j, RHS, stride=NZ * nx), :]
        bx[s, 32] = by[0, g]
        bx[s, 33] = by[1, g]
        for z in range(NZ):
            bx[s, 34 + z] = c_ref[z, 8 * t : 8 * t + 8, :]
            bx[s, 42 + z] = r_ref[z, 8 * t : 8 * t + 8, :]
        for i in range(2):
            bx[s, 50 + i] = by[0, groups + tiles * i + t]
        for side in range(2):
            bd[s, side, 0] = by[side, g]
            bd[s, side, 1] = by[0, groups + t]
            bd[s, side, 2] = by[0, groups + tiles + t]


def swap_kernel(gx, gy, bx, by, bd, rx, ry, rd, send, recv):
    mx, my = lax.axis_index("gx"), lax.axis_index("gy")
    xs = (lax.rem(mx + gx - 1, gx), lax.rem(mx + 1, gx))
    ys = (lax.rem(my + gy - 1, gy), lax.rem(my + 1, gy))
    jobs = []
    for s in range(2):
        jobs.append((bx.at[s], rx.at[1 - s], (xs[s], my)))
    for s in range(2):
        jobs.append((by.at[s], ry.at[1 - s], (mx, ys[s])))
    for s in range(2):
        for t in range(2):
            jobs.append((bd.at[s, t], rd.at[1 - s, 1 - t], (xs[s], ys[t])))
    barrier = pltpu.get_barrier_semaphore()
    for _, _, where in jobs:
        pl.semaphore_signal(barrier, inc=1, device_id=where, device_id_type=MESH)
    pl.semaphore_wait(barrier, len(jobs))
    copies = []
    for i, (src, dst, where) in enumerate(jobs):
        copy = pltpu.make_async_remote_copy(
            src_ref=src, dst_ref=dst, send_sem=send.at[i], recv_sem=recv.at[i],
            device_id=where, device_id_type=MESH)
        copy.start()
        copies.append(copy)
    for copy in copies:
        copy.wait()


def split3(a):
    high = a.astype(BF16).astype(F32)
    rest = a - high
    mid = rest.astype(BF16).astype(F32)
    return high, mid, rest - mid


def gram_add(acc, a):
    s = jnp.concatenate(split3(a), 0).astype(BF16)
    acc[...] += lax.dot_general(s, s, (((1,), (1,)), ((), ())), preferred_element_type=F32)


def gram_fold(acc):
    rows = acc[0:COLS, :] + acc[COLS : 2 * COLS, :] + acc[2 * COLS :, :]
    g = rows[:, 0:COLS] + rows[:, COLS : 2 * COLS] + rows[:, 2 * COLS :]
    g = jnp.concatenate([g, jnp.zeros((COLS, LANES - COLS), F32)], 1)
    last = jnp.concatenate([g[32:40], jnp.zeros((8, LANES), F32)], 0)
    return g[0:16] + roll(g[16:32], 40) + roll(last, 80)


def factor(packed, cells):
    g = jnp.concatenate([packed, roll(packed, -40), roll(packed[0:8], -80)], 0) * (1.0 / cells)
    lane = lane_iota((COLS, LANES))
    row = lax.broadcasted_iota(jnp.int32, (COLS, LANES), 0)
    m = jnp.where(lane < COLS, g, jnp.where(lane - 64 == row, 1.0, 0.0))
    row1 = lax.broadcasted_iota(jnp.int32, (COLS, 1), 0)
    for j in range(COLS - 1):
        pivot = m[j : j + 1, :]
        scaled = pivot * (1.0 / m[j : j + 1, j : j + 1])
        f = jnp.where(row1 > j, m[:, j : j + 1], 0.0)
        m = m - f * scaled
    d = jnp.sum(jnp.where(lane == row, m, 0.0), axis=1, keepdims=True)
    m = m * (1.0 / jnp.sqrt(d))
    upper = jnp.where((lane >= row) & (lane < COLS), m, 0.0)
    inverse = jnp.where(lane <= row, roll(m, 64), 0.0)
    return upper[:, :COLS], inverse[:, :COLS]


def stack_left(matrix):
    h, m, l = split3(matrix)
    return jnp.concatenate([h, h, m, m, h, l], 1).astype(BF16)


def times(left, a):
    h, m, l = split3(a)
    hm = jnp.concatenate([h, m], 0).astype(BF16)
    lh = jnp.concatenate([l, h], 0).astype(BF16)
    return jnp.dot(left, jnp.concatenate([hm, hm, lh], 0), preferred_element_type=F32)


def across(ref, rows):
    return jnp.concatenate([ref[i, z] for i in rows for z in range(NZ)], 1)


def rows_at_once(count, most):
    return max(n for n in range(1, most + 1) if count % n == 0)


def power_kernel(nx, u_ref, c_ref, r_ref, by, rx, ry, rd, out, gp, kb, cb, rb, w, cs, sw, sb, fl, acc, sem):
    ext = nx + 8
    groups = nx // 4
    tiles = nx // 8
    lane = lane_iota((8, LANES))
    lane1 = lane_iota((1, LANES))
    sub = (lane % 16) // 4
    u2 = u_ref.reshape(RHS * NZ * nx, LANES)
    c2 = c_ref.reshape(NZ * nx, LANES)
    r2 = r_ref.reshape(NZ * nx, LANES)
    rx2 = rx.reshape(2 * 52 * 8, LANES)
    W = THIRD * 0.5

    for i, dst in ((0, cb), (1, rb)):
        for k in range(4):
            base = (34 + 8 * i) * 8
            dst[k] = rx2[pl.ds(base + 4 + k, 8, stride=8), :]
            dst[nx + 4 + k] = rx2[pl.ds(52 * 8 + base + k, 8, stride=8), :]

    def coef(i, _):
        xs = [4 * i + k for k in range(4)]
        cr = [(c2[pl.ds(x, 8, stride=nx), :], r2[pl.ds(x, 8, stride=nx), :]) for x in xs]
        us = [[u2[pl.ds(z * nx + x, RHS, stride=NZ * nx), :] for z in range(NZ)] for x in xs]
        for k, x in enumerate(xs):
            cb[x + 4] = cr[k][0]
            rb[x + 4] = cr[k][1]
            for z in range(NZ):
                kb[x + 4, z, 0:RHS, :] = us[k][z]
        return 0

    lax.fori_loop(0, nx // 4, coef, 0)
    for j in range(4):
        for z in range(NZ):
            kb[j, z, 0:RHS, :] = rx[0, j * 8 + z]
            kb[nx + 4 + j, z, 0:RHS, :] = rx[1, j * 8 + z]

    w[1, 0] = (cb[0] + cb[1]) * W

    many = rows_at_once(ext - 2, 10)

    def weight(i, _):
        out = []
        for k in range(many):
            x = 1 + i * many + k
            c = cb[x]
            xp, xm = (c + cb[x + 1]) * W, (c + cb[x - 1]) * W
            zp = (c + roll(c, -1, 0)) * W
            yp = jnp.where(lane == LANES - 1, 0.0, (c + roll(c, -1)) * W)
            zm = roll(zp, 1, 0)
            ym = jnp.where(lane == 0, 0.0, (c + roll(c, 1)) * W)
            diag = (rb[x] - CENTER_SHIFT) * THIRD + (xp + xm + zp + zm + yp + ym)
            out.append((diag, xp, yp, ym, zp, zm))
        for k in range(many):
            for n in range(6):
                w[n, 1 + i * many + k] = out[k][n]
        return 0

    lax.fori_loop(0, (ext - 2) // many, weight, 0)

    for i in range(2):
        cs[i, 0:8, :] = jnp.zeros((8, LANES), F32)
        cs[i, nx + 24 : nx + 32, :] = jnp.zeros((8, LANES), F32)
        for t in range(tiles + 2):
            if t == 0 or t == tiles + 1:
                s = 0 if t == 0 else 1
                own, left, right = rx[s, 50 + i], rd[s, 0, 1 + i], rd[s, 1, 1 + i]
            else:
                at = groups + tiles * i + t - 1
                own, left, right = by[0, at], ry[0, at], ry[1, at]
            cs[i, 8 + 8 * t : 16 + 8 * t, :] = jnp.where(
                sub == 0, roll(left, -8), jnp.where(sub == 3, roll(right, 8), own))
    for t in range(tiles + 2):
        a = 8 + 8 * t
        c = cs[0, a : a + 8, :]
        xp = (c + cs[0, a + 1 : a + 9, :]) * W
        xm = (c + cs[0, a - 1 : a + 7, :]) * W
        yp, ym = (c + roll(c, -1)) * W, (c + roll(c, 1)) * W
        zp, zm = (c + roll(c, -16)) * W, (c + roll(c, 16)) * W
        total = xp + xm + zp + zm + yp + ym
        sw[0, a : a + 8, :] = (cs[1, a : a + 8, :] - CENTER_SHIFT) * THIRD + total
        for k, value in enumerate((xp, xm, yp, ym, zp, zm)):
            sw[1 + k, a : a + 8, :] = value

    def strip(g, parts):
        left, own_left, own_right, right = parts
        for j in range(4):
            v = jnp.where(sub == 0, roll(left, -4 * j), roll(own_left, 4 - 4 * j))
            v = jnp.where(sub == 2, roll(own_right, 8 - 4 * j), v)
            sb[0, 4 * g + j] = jnp.where(sub == 3, roll(right, 12 - 4 * j), v)

    strip(0, (rd[0, 0, 0], rx[0, 32], rx[0, 33], rd[0, 1, 0]))
    strip(groups + 1, (rd[1, 0, 0], rx[1, 32], rx[1, 33], rd[1, 1, 0]))

    def strips(g, _):
        strip(g, (ry[0, g - 1], by[0, g - 1], by[1, g - 1], ry[1, g - 1]))
        return 0

    lax.fori_loop(1, groups + 1, strips, 0)

    for p in range(STEPS):
        size = rows_at_once(ext - 2 * p - 2, 17)

        def strip_rows(i, _):
            fluxes, nexts = [], []
            for k in range(size):
                x = p + 1 + i * size + k
                s = sb[p, x]

                def wt(n):
                    return sw[n, pl.ds(x + 12, 1), :]

                sr, sl = roll(s, -1), roll(s, 1)
                wr, wl = wt(3), wt(4)
                fluxes.append(jnp.where(lane % 16 == 11, wr * (sr - s), roll(wl * (sl - s), 8)))
                if p < STEPS - 1:
                    ax = wt(1) * sb[p, x + 1] + wt(2) * sb[p, x - 1]
                    az = wt(5) * roll(s, -16) + wt(6) * roll(s, 16)
                    nexts.append((wt(0) * s - ax) - ((wr * sr + wl * sl) + az))
            for k in range(size):
                x = p + 1 + i * size + k
                fl[p, x] = fluxes[k]
                if p < STEPS - 1:
                    sb[p + 1, x] = nexts[k]
            return 0

        lax.fori_loop(0, (ext - 2 * p - 2) // size, strip_rows, 0)

    acc[...] = jnp.zeros_like(acc)
    edge = (lane == 0) | (lane == LANES - 1)

    def leave(i, count):
        return pltpu.make_async_copy(
            kb.at[pl.ds(4 + i * count, count)], out.at[pl.ds(i * count, count)], sem.at[i])

    for p in range(1, STEPS + 1):
        lo, hi = RHS * (p - 1), RHS * p
        count = rows_at_once(ext - 2 * p, 5)

        def rows(i, _):
            first = p + i * count
            news = {}
            for k in range(count):
                x = first + k
                cen = [kb[x, z, lo:hi, :] for z in range(NZ)]
                flux = fl[p - 1, x]
                for z in range(NZ):
                    c = cen[z]

                    def wt(n, at):
                        return w[n, at, z : z + 1, :]

                    mid = wt(0, x) * c - jnp.where(edge, roll(flux, 116 - 16 * z), 0.0)
                    ax = wt(1, x) * kb[x + 1, z, lo:hi, :] + wt(1, x - 1) * kb[x - 1, z, lo:hi, :]
                    ay = wt(2, x) * roll(c, -1) + wt(3, x) * roll(c, 1)
                    az = wt(4, x) * cen[(z + 1) % NZ] + wt(5, x) * cen[(z - 1) % NZ]
                    news[k, z] = (mid - ax) - (ay + az)
            for k in range(count):
                for z in range(NZ):
                    kb[first + k, z, hi : hi + RHS, :] = news[k, z]
            if p == STEPS:
                leave(i, count).start()
                gram_add(acc, across(kb, [first + k for k in range(count)]))
            return 0

        lax.fori_loop(0, (ext - 2 * p) // count, rows, 0)
    gp[...] = gram_fold(acc)
    for i in range(nx // 4):
        leave(i, 4).wait()


def sum_kernel(gx, gy, g_ref, out, bufx, bufy, sx, rx, sy, ry):
    mx, my = lax.axis_index("gx"), lax.axis_index("gy")
    barrier = pltpu.get_barrier_semaphore()
    xs = [lax.rem(mx + d, gx) for d in range(1, gx)]
    ys = [lax.rem(my + d, gy) for d in range(1, gy)]
    for x in xs:
        pl.semaphore_signal(barrier, inc=1, device_id=(x, my), device_id_type=MESH)
    for y in ys:
        pl.semaphore_signal(barrier, inc=1, device_id=(mx, y), device_id_type=MESH)
    pl.semaphore_wait(barrier, len(xs) + len(ys))

    def stage(source, buf, send, recv, me, n, peers, where):
        copies = []
        for i, peer in enumerate(peers):
            copy = pltpu.make_async_remote_copy(
                src_ref=source, dst_ref=buf.at[me], send_sem=send.at[i],
                recv_sem=recv.at[i], device_id=where(peer), device_id_type=MESH)
            copy.start()
            copies.append(copy)
        buf[me] = source[...]
        for copy in copies:
            copy.wait()
        total = buf[0]
        for i in range(1, n):
            total = total + buf[i]
        return total

    out[...] = stage(g_ref, bufx, sx, rx, mx, gx, xs, lambda x: (x, my))
    out[...] = stage(out, bufy, sy, ry, my, gy, ys, lambda y: (mx, y))


def all_sum(packed, gx, gy, cid):
    return pl.pallas_call(
        functools.partial(sum_kernel, gx, gy),
        out_shape=jax.ShapeDtypeStruct(packed.shape, F32),
        in_specs=[VM],
        out_specs=VM,
        scratch_shapes=[
            pltpu.VMEM((gx,) + packed.shape, F32),
            pltpu.VMEM((gy,) + packed.shape, F32),
            pltpu.SemaphoreType.DMA((gx - 1,)),
            pltpu.SemaphoreType.DMA((gx - 1,)),
            pltpu.SemaphoreType.DMA((gy - 1,)),
            pltpu.SemaphoreType.DMA((gy - 1,)),
        ],
        compiler_params=pltpu.CompilerParams(collective_id=cid, has_side_effects=True),
        name=f"sum_{cid}",
    )(packed)


def again_kernel(cells, steps, g_ref, k_ref, upper, inverse, gp, left, acc):
    i = pl.program_id(0)

    @pl.when(i == 0)
    def _():
        up, inv = factor(g_ref[...], cells)
        upper[...] = up
        inverse[...] = inv
        left[...] = stack_left(inv)
        acc[...] = jnp.zeros_like(acc)

    gram_add(acc, times(left[...], across(k_ref, range(k_ref.shape[0]))))

    @pl.when(i == steps - 1)
    def _():
        gp[...] = gram_fold(acc)


def basis_kernel(cells, g_ref, up_ref, inv_ref, k_ref, out, r_out, left):
    @pl.when(pl.program_id(0) == 0)
    def _():
        up, inv = factor(g_ref[...], cells)
        r_out[...] = jnp.dot(up, up_ref[...], precision=lax.Precision.HIGHEST, preferred_element_type=F32)
        both = jnp.dot(inv, inv_ref[...], precision=lax.Precision.HIGHEST, preferred_element_type=F32)
        left[...] = stack_left(both)

    flat = out.reshape(COLS * NZ * 8, LANES)
    for x in range(8):
        q = times(left[...], across(k_ref, [x]))
        for z in range(NZ):
            for b in range(COLS // 8):
                flat[pl.ds(b * 8 * NZ * 8 + z * 8 + x, 8, stride=NZ * 8), :] = q[
                    8 * b : 8 * b + 8, LANES * z : LANES * (z + 1)]


def body(start_block, conductivity, reaction):
    gx, gy = lax.axis_size("gx"), lax.axis_size("gy")
    nx = start_block.shape[2]
    ext = nx + 8
    cells = NZ * nx * LANES * gx * gy
    sds = lambda *s: jax.ShapeDtypeStruct(s, F32)
    shapes = [sds(2, 52, 8, LANES), sds(2, nx // 4 + nx // 4, 8, LANES), sds(2, 2, 3, 8, LANES)]
    big = pltpu.CompilerParams(vmem_limit_bytes=48 * 2**20)
    bx, by, bd = pl.pallas_call(
        functools.partial(pack_kernel, nx), out_shape=shapes,
        in_specs=[VM] * 3, out_specs=[VM] * 3, compiler_params=big, name="pack",
    )(start_block, conductivity, reaction)
    rx, ry, rd = pl.pallas_call(
        functools.partial(swap_kernel, gx, gy), out_shape=shapes,
        in_specs=[VM] * 3, out_specs=[VM] * 3,
        scratch_shapes=[pltpu.SemaphoreType.DMA((8,)), pltpu.SemaphoreType.DMA((8,))],
        compiler_params=pltpu.CompilerParams(collective_id=0, has_side_effects=True), name="swap",
    )(bx, by, bd)
    kb, gp = pl.pallas_call(
        functools.partial(power_kernel, nx),
        out_shape=[sds(nx, NZ, COLS, LANES), sds(16, LANES)],
        in_specs=[VM] * 7, out_specs=[pl.BlockSpec(memory_space=pl.ANY), VM],
        scratch_shapes=[
            pltpu.VMEM((ext, NZ, COLS, LANES), F32),
            pltpu.VMEM((ext, 8, LANES), F32),
            pltpu.VMEM((ext, 8, LANES), F32),
            pltpu.VMEM((6, ext, 8, LANES), F32),
            pltpu.VMEM((2, nx + 32, LANES), F32),
            pltpu.VMEM((7, nx + 32, LANES), F32),
            pltpu.VMEM((STEPS, ext, 8, LANES), F32),
            pltpu.VMEM((STEPS, ext, 8, LANES), F32),
            pltpu.VMEM((3 * COLS, 3 * COLS), F32),
            pltpu.SemaphoreType.DMA((nx // 4,)),
        ],
        compiler_params=big, name="powers",
    )(start_block, conductivity, reaction, by, rx, ry, rd)
    total = all_sum(gp, gx, gy, 1)

    whole = lambda *s: pl.BlockSpec(s, lambda i: (0,) * len(s))
    kblock = lambda n: pl.BlockSpec((n, NZ, COLS, LANES), lambda i: (i, 0, 0, 0))
    steps = nx // 4
    upper, inverse, gp2 = pl.pallas_call(
        functools.partial(again_kernel, cells, steps),
        grid=(steps,),
        out_shape=[sds(COLS, COLS), sds(COLS, COLS), sds(16, LANES)],
        in_specs=[whole(16, LANES), kblock(4)],
        out_specs=[whole(COLS, COLS), whole(COLS, COLS), whole(16, LANES)],
        scratch_shapes=[pltpu.VMEM((COLS, 6 * COLS), BF16), pltpu.VMEM((3 * COLS, 3 * COLS), F32)],
        compiler_params=big, name="again",
    )(total, kb)
    total2 = all_sum(gp2, gx, gy, 2)
    basis, r_factor = pl.pallas_call(
        functools.partial(basis_kernel, cells),
        grid=(nx // 8,),
        out_shape=[sds(COLS, NZ, nx, LANES), sds(COLS, COLS)],
        in_specs=[whole(16, LANES), whole(COLS, COLS), whole(COLS, COLS),
                  kblock(8)],
        out_specs=[pl.BlockSpec((COLS, NZ, 8, LANES), lambda i: (0, 0, i, 0)), whole(COLS, COLS)],
        scratch_shapes=[pltpu.VMEM((COLS, 6 * COLS), BF16)],
        compiler_params=big, name="basis",
    )(total2, upper, inverse, kb)
    return basis, r_factor, upper


def solution(mesh):
    return jax.shard_map(
        body,
        mesh=mesh,
        in_specs=(P(None, None, "gx", "gy"), P(None, "gx", "gy"), P(None, "gx", "gy")),
        out_specs=(P(None, None, "gx", "gy"), P(), P()),
        check_vma=False,
    )
```

```python
import functools

import jax
import jax.numpy as jnp
from jax import lax
from jax.experimental import pallas as pl
from jax.experimental.pallas import tpu as pltpu
from jax.sharding import PartitionSpec as P

STEPS = 4
RHS = 8
NZ = 8
COLS = RHS * (STEPS + 1)
LANES = 128
CENTER_SHIFT = 7.0
THIRD = 1.0 / 3.0
MESH = pl.DeviceIdType.MESH
VM = pl.BlockSpec(memory_space=pltpu.VMEM)
F32 = jnp.float32
BF16 = jnp.bfloat16


def lane_iota(shape):
    return lax.broadcasted_iota(jnp.int32, shape, len(shape) - 1)


def roll(v, shift, axis=1):
    shift = shift % v.shape[axis]
    return v if shift == 0 else pltpu.roll(v, shift, axis)


def pack_kernel(nx, u_ref, c_ref, r_ref, bx, by, bd):
    u2 = u_ref.reshape(RHS * NZ * nx, LANES)
    quad = lane_iota((8, LANES)) // 4
    groups = nx // 4
    tiles = nx // 8

    def group(g, _):
        left = jnp.zeros((8, LANES), F32)
        right = jnp.zeros((8, LANES), F32)
        for j in range(4):
            for z in range(NZ):
                v = u2[pl.ds(z * nx + 4 * g + j, RHS, stride=NZ * nx), :]
                here = quad == 4 * z + j
                left = jnp.where(here, roll(v, 16 * z + 4 * j), left)
                right = jnp.where(here, roll(v, 16 * z + 4 * j + 4), right)
        by[0, g] = left
        by[1, g] = right
        return 0

    lax.fori_loop(0, groups, group, 0)
    for i, ref in enumerate((c_ref, r_ref)):
        for t in range(tiles):
            edge = jnp.zeros((8, LANES), F32)
            for z in range(NZ):
                v = ref[z, 8 * t : 8 * t + 8, :]
                edge = jnp.where(quad == 4 * z + 1, roll(v, 16 * z + 4), edge)
                edge = jnp.where(quad == 4 * z + 2, roll(v, 16 * z + 12), edge)
            by[0, groups + tiles * i + t] = edge
            by[1, groups + tiles * i + t] = edge
    for s in range(2):
        g, t, base = (0, 0, 0) if s == 0 else (groups - 1, tiles - 1, nx - 4)
        for j in range(4):
            for z in range(NZ):
                bx[s, j * 8 + z] = u2[pl.ds(z * nx + base + j, RHS, stride=NZ * nx), :]
        bx[s, 32] = by[0, g]
        bx[s, 33] = by[1, g]
        for z in range(NZ):
            bx[s, 34 + z] = c_ref[z, 8 * t : 8 * t + 8, :]
            bx[s, 42 + z] = r_ref[z, 8 * t : 8 * t + 8, :]
        for i in range(2):
            bx[s, 50 + i] = by[0, groups + tiles * i + t]
        for side in range(2):
            bd[s, side, 0] = by[side, g]
            bd[s, side, 1] = by[0, groups + t]
            bd[s, side, 2] = by[0, groups + tiles + t]


def swap_kernel(gx, gy, bx, by, bd, rx, ry, rd, send, recv):
    mx, my = lax.axis_index("gx"), lax.axis_index("gy")
    xs = (lax.rem(mx + gx - 1, gx), lax.rem(mx + 1, gx))
    ys = (lax.rem(my + gy - 1, gy), lax.rem(my + 1, gy))
    jobs = []
    for s in range(2):
        jobs.append((bx.at[s], rx.at[1 - s], (xs[s], my)))
    for s in range(2):
        jobs.append((by.at[s], ry.at[1 - s], (mx, ys[s])))
    for s in range(2):
        for t in range(2):
            jobs.append((bd.at[s, t], rd.at[1 - s, 1 - t], (xs[s], ys[t])))
    barrier = pltpu.get_barrier_semaphore()
    for _, _, where in jobs:
        pl.semaphore_signal(barrier, inc=1, device_id=where, device_id_type=MESH)
    pl.semaphore_wait(barrier, len(jobs))
    copies = []
    for i, (src, dst, where) in enumerate(jobs):
        copy = pltpu.make_async_remote_copy(
            src_ref=src, dst_ref=dst, send_sem=send.at[i], recv_sem=recv.at[i],
            device_id=where, device_id_type=MESH)
        copy.start()
        copies.append(copy)
    for copy in copies:
        copy.wait()


def split3(a):
    high = a.astype(BF16).astype(F32)
    rest = a - high
    mid = rest.astype(BF16).astype(F32)
    return high, mid, rest - mid


def gram_add(acc, a):
    s = jnp.concatenate(split3(a), 0).astype(BF16)
    acc[...] += lax.dot_general(s, s, (((1,), (1,)), ((), ())), preferred_element_type=F32)


def gram_fold(acc):
    rows = acc[0:COLS, :] + acc[COLS : 2 * COLS, :] + acc[2 * COLS :, :]
    g = rows[:, 0:COLS] + rows[:, COLS : 2 * COLS] + rows[:, 2 * COLS :]
    g = jnp.concatenate([g, jnp.zeros((COLS, LANES - COLS), F32)], 1)
    last = jnp.concatenate([g[32:40], jnp.zeros((8, LANES), F32)], 0)
    return g[0:16] + roll(g[16:32], 40) + roll(last, 80)


def factor(packed, cells):
    g = jnp.concatenate([packed, roll(packed, -40), roll(packed[0:8], -80)], 0) * (1.0 / cells)
    lane = lane_iota((COLS, LANES))
    row = lax.broadcasted_iota(jnp.int32, (COLS, LANES), 0)
    m = jnp.where(lane < COLS, g, jnp.where(lane - 64 == row, 1.0, 0.0))
    row1 = lax.broadcasted_iota(jnp.int32, (COLS, 1), 0)
    for j in range(COLS - 1):
        pivot = m[j : j + 1, :]
        scaled = pivot * (1.0 / m[j : j + 1, j : j + 1])
        f = jnp.where(row1 > j, m[:, j : j + 1], 0.0)
        m = m - f * scaled
    d = jnp.sum(jnp.where(lane == row, m, 0.0), axis=1, keepdims=True)
    m = m * (1.0 / jnp.sqrt(d))
    upper = jnp.where((lane >= row) & (lane < COLS), m, 0.0)
    inverse = jnp.where(lane <= row, roll(m, 64), 0.0)
    return upper[:, :COLS], inverse[:, :COLS]


def stack_left(matrix):
    h, m, l = split3(matrix)
    return jnp.concatenate([h, h, m, m, h, l], 1).astype(BF16)


def times(left, a):
    h, m, l = split3(a)
    hm = jnp.concatenate([h, m], 0).astype(BF16)
    lh = jnp.concatenate([l, h], 0).astype(BF16)
    return jnp.dot(left, jnp.concatenate([hm, hm, lh], 0), preferred_element_type=F32)


def across(ref, rows):
    return jnp.concatenate([ref[i, z] for i in rows for z in range(NZ)], 1)


def rows_at_once(count, most):
    return max(n for n in range(1, most + 1) if count % n == 0)


def power_kernel(nx, u_ref, c_ref, r_ref, by, rx, ry, rd, out, gp, kb, cb, rb, w, cs, sw, sb, fl, acc, sem):
    ext = nx + 8
    groups = nx // 4
    tiles = nx // 8
    lane = lane_iota((8, LANES))
    lane1 = lane_iota((1, LANES))
    sub = (lane % 16) // 4
    u2 = u_ref.reshape(RHS * NZ * nx, LANES)
    c2 = c_ref.reshape(NZ * nx, LANES)
    r2 = r_ref.reshape(NZ * nx, LANES)
    rx2 = rx.reshape(2 * 52 * 8, LANES)
    W = THIRD * 0.5

    for i, dst in ((0, cb), (1, rb)):
        for k in range(4):
            base = (34 + 8 * i) * 8
            dst[k] = rx2[pl.ds(base + 4 + k, 8, stride=8), :]
            dst[nx + 4 + k] = rx2[pl.ds(52 * 8 + base + k, 8, stride=8), :]

    def coef(i, _):
        xs = [4 * i + k for k in range(4)]
        cr = [(c2[pl.ds(x, 8, stride=nx), :], r2[pl.ds(x, 8, stride=nx), :]) for x in xs]
        us = [[u2[pl.ds(z * nx + x, RHS, stride=NZ * nx), :] for z in range(NZ)] for x in xs]
        for k, x in enumerate(xs):
            cb[x + 4] = cr[k][0]
            rb[x + 4] = cr[k][1]
            for z in range(NZ):
                kb[x + 4, z, 0:RHS, :] = us[k][z]
        return 0

    lax.fori_loop(0, nx // 4, coef, 0)
    for j in range(4):
        for z in range(NZ):
            kb[j, z, 0:RHS, :] = rx[0, j * 8 + z]
            kb[nx + 4 + j, z, 0:RHS, :] = rx[1, j * 8 + z]

    w[1, 0] = (cb[0] + cb[1]) * W

    many = rows_at_once(ext - 2, 10)

    def weight(i, _):
        out = []
        for k in range(many):
            x = 1 + i * many + k
            c = cb[x]
            xp, xm = (c + cb[x + 1]) * W, (c + cb[x - 1]) * W
            zp = (c + roll(c, -1, 0)) * W
            yp = jnp.where(lane == LANES - 1, 0.0, (c + roll(c, -1)) * W)
            zm = roll(zp, 1, 0)
            ym = jnp.where(lane == 0, 0.0, (c + roll(c, 1)) * W)
            diag = (rb[x] - CENTER_SHIFT) * THIRD + (xp + xm + zp + zm + yp + ym)
            out.append((diag, xp, yp, ym, zp, zm))
        for k in range(many):
            for n in range(6):
                w[n, 1 + i * many + k] = out[k][n]
        return 0

    lax.fori_loop(0, (ext - 2) // many, weight, 0)

    for i in range(2):
        cs[i, 0:8, :] = jnp.zeros((8, LANES), F32)
        cs[i, nx + 24 : nx + 32, :] = jnp.zeros((8, LANES), F32)
        for t in range(tiles + 2):
            if t == 0 or t == tiles + 1:
                s = 0 if t == 0 else 1
                own, left, right = rx[s, 50 + i], rd[s, 0, 1 + i], rd[s, 1, 1 + i]
            else:
                at = groups + tiles * i + t - 1
                own, left, right = by[0, at], ry[0, at], ry[1, at]
            cs[i, 8 + 8 * t : 16 + 8 * t, :] = jnp.where(
                sub == 0, roll(left, -8), jnp.where(sub == 3, roll(right, 8), own))
    for t in range(tiles + 2):
        a = 8 + 8 * t
        c = cs[0, a : a + 8, :]
        xp = (c + cs[0, a + 1 : a + 9, :]) * W
        xm = (c + cs[0, a - 1 : a + 7, :]) * W
        yp, ym = (c + roll(c, -1)) * W, (c + roll(c, 1)) * W
        zp, zm = (c + roll(c, -16)) * W, (c + roll(c, 16)) * W
        total = xp + xm + zp + zm + yp + ym
        sw[0, a : a + 8, :] = (cs[1, a : a + 8, :] - CENTER_SHIFT) * THIRD + total
        for k, value in enumerate((xp, xm, yp, ym, zp, zm)):
            sw[1 + k, a : a + 8, :] = value

    def strip(g, parts):
        left, own_left, own_right, right = parts
        for j in range(4):
            v = jnp.where(sub == 0, roll(left, -4 * j), roll(own_left, 4 - 4 * j))
            v = jnp.where(sub == 2, roll(own_right, 8 - 4 * j), v)
            sb[0, 4 * g + j] = jnp.where(sub == 3, roll(right, 12 - 4 * j), v)

    strip(0, (rd[0, 0, 0], rx[0, 32], rx[0, 33], rd[0, 1, 0]))
    strip(groups + 1, (rd[1, 0, 0], rx[1, 32], rx[1, 33], rd[1, 1, 0]))

    def strips(g, _):
        strip(g, (ry[0, g - 1], by[0, g - 1], by[1, g - 1], ry[1, g - 1]))
        return 0

    lax.fori_loop(1, groups + 1, strips, 0)

    for p in range(STEPS):
        size = rows_at_once(ext - 2 * p - 2, 17)

        def strip_rows(i, _):
            fluxes, nexts = [], []
            for k in range(size):
                x = p + 1 + i * size + k
                s = sb[p, x]

                def wt(n):
                    return sw[n, pl.ds(x + 12, 1), :]

                sr, sl = roll(s, -1), roll(s, 1)
                wr, wl = wt(3), wt(4)
                fluxes.append(jnp.where(lane % 16 == 11, wr * (sr - s), roll(wl * (sl - s), 8)))
                if p < STEPS - 1:
                    ax = wt(1) * sb[p, x + 1] + wt(2) * sb[p, x - 1]
                    az = wt(5) * roll(s, -16) + wt(6) * roll(s, 16)
                    nexts.append((wt(0) * s - ax) - ((wr * sr + wl * sl) + az))
            for k in range(size):
                x = p + 1 + i * size + k
                fl[p, x] = fluxes[k]
                if p < STEPS - 1:
                    sb[p + 1, x] = nexts[k]
            return 0

        lax.fori_loop(0, (ext - 2 * p - 2) // size, strip_rows, 0)

    acc[...] = jnp.zeros_like(acc)
    edge = (lane == 0) | (lane == LANES - 1)

    def leave(i, count):
        return pltpu.make_async_copy(
            kb.at[pl.ds(4 + i * count, count)], out.at[pl.ds(i * count, count)], sem.at[i])

    for p in range(1, STEPS + 1):
        lo, hi = RHS * (p - 1), RHS * p
        count = 4 if p == STEPS else rows_at_once(ext - 2 * p, 6)

        def rows(i, _):
            first = p + i * count
            news = {}
            for k in range(count):
                x = first + k
                cen = [kb[x, z, lo:hi, :] for z in range(NZ)]
                flux = fl[p - 1, x]
                for z in range(NZ):
                    c = cen[z]

                    def wt(n, at):
                        return w[n, at, z : z + 1, :]

                    mid = wt(0, x) * c - jnp.where(edge, roll(flux, 116 - 16 * z), 0.0)
                    ax = wt(1, x) * kb[x + 1, z, lo:hi, :] + wt(1, x - 1) * kb[x - 1, z, lo:hi, :]
                    ay = wt(2, x) * roll(c, -1) + wt(3, x) * roll(c, 1)
                    az = wt(4, x) * cen[(z + 1) % NZ] + wt(5, x) * cen[(z - 1) % NZ]
                    news[k, z] = (mid - ax) - (ay + az)
            for k in range(count):
                for z in range(NZ):
                    kb[first + k, z, hi : hi + RHS, :] = news[k, z]
            if p == STEPS:
                leave(i, count).start()
                gram_add(acc, across(kb, [first + k for k in range(count)]))
            return 0

        lax.fori_loop(0, (ext - 2 * p) // count, rows, 0)
    gp[...] = gram_fold(acc)
    for i in range(nx // 4):
        leave(i, 4).wait()


def sum_kernel(gx, gy, g_ref, out, bufx, bufy, sx, rx, sy, ry):
    mx, my = lax.axis_index("gx"), lax.axis_index("gy")
    barrier = pltpu.get_barrier_semaphore()
    xs = [lax.rem(mx + d, gx) for d in range(1, gx)]
    ys = [lax.rem(my + d, gy) for d in range(1, gy)]
    for x in xs:
        pl.semaphore_signal(barrier, inc=1, device_id=(x, my), device_id_type=MESH)
    for y in ys:
        pl.semaphore_signal(barrier, inc=1, device_id=(mx, y), device_id_type=MESH)
    pl.semaphore_wait(barrier, len(xs) + len(ys))

    def stage(source, buf, send, recv, me, n, peers, where):
        copies = []
        for i, peer in enumerate(peers):
            copy = pltpu.make_async_remote_copy(
                src_ref=source, dst_ref=buf.at[me], send_sem=send.at[i],
                recv_sem=recv.at[i], device_id=where(peer), device_id_type=MESH)
            copy.start()
            copies.append(copy)
        buf[me] = source[...]
        for copy in copies:
            copy.wait()
        total = buf[0]
        for i in range(1, n):
            total = total + buf[i]
        return total

    out[...] = stage(g_ref, bufx, sx, rx, mx, gx, xs, lambda x: (x, my))
    out[...] = stage(out, bufy, sy, ry, my, gy, ys, lambda y: (mx, y))


def all_sum(packed, gx, gy, cid):
    return pl.pallas_call(
        functools.partial(sum_kernel, gx, gy),
        out_shape=jax.ShapeDtypeStruct(packed.shape, F32),
        in_specs=[VM],
        out_specs=VM,
        scratch_shapes=[
            pltpu.VMEM((gx,) + packed.shape, F32),
            pltpu.VMEM((gy,) + packed.shape, F32),
            pltpu.SemaphoreType.DMA((gx - 1,)),
            pltpu.SemaphoreType.DMA((gx - 1,)),
            pltpu.SemaphoreType.DMA((gy - 1,)),
            pltpu.SemaphoreType.DMA((gy - 1,)),
        ],
        compiler_params=pltpu.CompilerParams(collective_id=cid, has_side_effects=True),
        name=f"sum_{cid}",
    )(packed)


def again_kernel(cells, steps, g_ref, k_ref, upper, inverse, gp, left, acc):
    i = pl.program_id(0)

    @pl.when(i == 0)
    def _():
        up, inv = factor(g_ref[...], cells)
        upper[...] = up
        inverse[...] = inv
        left[...] = stack_left(inv)
        acc[...] = jnp.zeros_like(acc)

    for first in range(0, k_ref.shape[0], 4):
        gram_add(acc, times(left[...], across(k_ref, range(first, first + 4))))

    @pl.when(i == steps - 1)
    def _():
        gp[...] = gram_fold(acc)


def basis_kernel(cells, g_ref, up_ref, inv_ref, k_ref, out, r_out, left):
    @pl.when(pl.program_id(0) == 0)
    def _():
        up, inv = factor(g_ref[...], cells)
        r_out[...] = jnp.dot(up, up_ref[...], precision=lax.Precision.HIGHEST, preferred_element_type=F32)
        both = jnp.dot(inv, inv_ref[...], precision=lax.Precision.HIGHEST, preferred_element_type=F32)
        left[...] = stack_left(both)

    flat = out.reshape(COLS * NZ * 8, LANES)
    for x in range(8):
        q = times(left[...], across(k_ref, [x]))
        for z in range(NZ):
            for b in range(COLS // 8):
                flat[pl.ds(b * 8 * NZ * 8 + z * 8 + x, 8, stride=NZ * 8), :] = q[
                    8 * b : 8 * b + 8, LANES * z : LANES * (z + 1)]


def body(start_block, conductivity, reaction):
    gx, gy = lax.axis_size("gx"), lax.axis_size("gy")
    nx = start_block.shape[2]
    ext = nx + 8
    cells = NZ * nx * LANES * gx * gy
    sds = lambda *s: jax.ShapeDtypeStruct(s, F32)
    shapes = [sds(2, 52, 8, LANES), sds(2, nx // 4 + nx // 4, 8, LANES), sds(2, 2, 3, 8, LANES)]
    big = pltpu.CompilerParams(vmem_limit_bytes=48 * 2**20)
    bx, by, bd = pl.pallas_call(
        functools.partial(pack_kernel, nx), out_shape=shapes,
        in_specs=[VM] * 3, out_specs=[VM] * 3, compiler_params=big, name="pack",
    )(start_block, conductivity, reaction)
    rx, ry, rd = pl.pallas_call(
        functools.partial(swap_kernel, gx, gy), out_shape=shapes,
        in_specs=[VM] * 3, out_specs=[VM] * 3,
        scratch_shapes=[pltpu.SemaphoreType.DMA((8,)), pltpu.SemaphoreType.DMA((8,))],
        compiler_params=pltpu.CompilerParams(collective_id=0, has_side_effects=True), name="swap",
    )(bx, by, bd)
    kb, gp = pl.pallas_call(
        functools.partial(power_kernel, nx),
        out_shape=[sds(nx, NZ, COLS, LANES), sds(16, LANES)],
        in_specs=[VM] * 7, out_specs=[pl.BlockSpec(memory_space=pl.ANY), VM],
        scratch_shapes=[
            pltpu.VMEM((ext, NZ, COLS, LANES), F32),
            pltpu.VMEM((ext, 8, LANES), F32),
            pltpu.VMEM((ext, 8, LANES), F32),
            pltpu.VMEM((6, ext, 8, LANES), F32),
            pltpu.VMEM((2, nx + 32, LANES), F32),
            pltpu.VMEM((7, nx + 32, LANES), F32),
            pltpu.VMEM((STEPS, ext, 8, LANES), F32),
            pltpu.VMEM((STEPS, ext, 8, LANES), F32),
            pltpu.VMEM((3 * COLS, 3 * COLS), F32),
            pltpu.SemaphoreType.DMA((nx // 4,)),
        ],
        compiler_params=big, name="powers",
    )(start_block, conductivity, reaction, by, rx, ry, rd)
    total = all_sum(gp, gx, gy, 1)

    whole = lambda *s: pl.BlockSpec(s, lambda i: (0,) * len(s))
    kblock = lambda n: pl.BlockSpec((n, NZ, COLS, LANES), lambda i: (i, 0, 0, 0))
    steps = nx // 8
    upper, inverse, gp2 = pl.pallas_call(
        functools.partial(again_kernel, cells, steps),
        grid=(steps,),
        out_shape=[sds(COLS, COLS), sds(COLS, COLS), sds(16, LANES)],
        in_specs=[whole(16, LANES), kblock(8)],
        out_specs=[whole(COLS, COLS), whole(COLS, COLS), whole(16, LANES)],
        scratch_shapes=[pltpu.VMEM((COLS, 6 * COLS), BF16), pltpu.VMEM((3 * COLS, 3 * COLS), F32)],
        compiler_params=big, name="again",
    )(total, kb)
    total2 = all_sum(gp2, gx, gy, 2)
    basis, r_factor = pl.pallas_call(
        functools.partial(basis_kernel, cells),
        grid=(nx // 8,),
        out_shape=[sds(COLS, NZ, nx, LANES), sds(COLS, COLS)],
        in_specs=[whole(16, LANES), whole(COLS, COLS), whole(COLS, COLS),
                  kblock(8)],
        out_specs=[pl.BlockSpec((COLS, NZ, 8, LANES), lambda i: (0, 0, i, 0)), whole(COLS, COLS)],
        scratch_shapes=[pltpu.VMEM((COLS, 6 * COLS), BF16)],
        compiler_params=big, name="basis",
    )(total2, upper, inverse, kb)
    return basis, r_factor, upper


def solution(mesh):
    return jax.shard_map(
        body,
        mesh=mesh,
        in_specs=(P(None, None, "gx", "gy"), P(None, "gx", "gy"), P(None, "gx", "gy")),
        out_specs=(P(None, None, "gx", "gy"), P(), P()),
        check_vma=False,
    )
```
